32 devices in a mesh: groups: 2 (over x), side: 16 (over z, y, core).
Axes of the slice: x: 2, y: 2, z: 4, core: 2. Of those that a mesh axis runs over, the one named last changes fastest.
Arguments:
- query: bfloat16 [256, 3072], P(('groups', 'side')), parts along dimension 0, may hold values from -48 to 48
- new_key: bfloat16 [256, 512], P(('groups', 'side')), parts along dimension 0, may hold values from -6 to 6
- new_value: bfloat16 [256, 512], P(('groups', 'side')), parts along dimension 0, may hold values from -6 to 6
- key_cache: bfloat16 [256, 128, 512], P(('groups', 'side')), parts along dimension 0, may hold values from -6 to 6
- value_cache: bfloat16 [256, 128, 512], P(('groups', 'side')), parts along dimension 0, may hold values from -6 to 6
- lengths: int32 [256], P(('groups', 'side')), parts along dimension 0, may hold values from 2 to 128
- residual: bfloat16 [256, 3072], P(('groups', 'side')), parts along dimension 0, may hold values from -6 to 6
- norm_gain: bfloat16 [3072], replicated, may hold values from 0.3984375 to 1.59375
- router: bfloat16 [3072, 8], replicated, may hold values from -0.109375 to 0.109375
- routes: int32 [256, 2], P(('groups', 'side')), parts along dimension 0, may hold values from 0 to 7, all different within a row; in each aligned block of 4 rows (0 to 3, 4 to 7, ...) at most 2 rows name the same one
- w_gate: bfloat16 [3072, 8192], P(None, 'side'), may hold values from -0.109375 to 0.109375
- w_up: bfloat16 [3072, 8192], P(None, 'side'), may hold values from -0.109375 to 0.109375
- w_down: bfloat16 [8192, 3072], P('side'), may hold values from -0.1875 to 0.1875
Outputs:
- layer_output: bfloat16 [256, 3072], P(('groups', 'side')), parts along dimension 0
The draws below stay inside these ranges and needn't reach their ends.
There are 2 independent parts, one for each index of `groups`. The reference program is written for one: setup_inputs(seed, part) draws one part's arguments, and reference() takes and returns one part's arrays. A program takes and returns all parts, laid end to end along the dimension named above; an argument that names none is the same for every part. Nothing has to cross between parts.
Inputs may be any that keep to these rules, and one draw needn't show every extreme that they name: `routes`: in each aligned block of 4 sequences (each half of one device's sequences) no expert is named by more than 2 of them.
All inputs are finite; a program needn't handle non-finite values.
Results may differ from the reference program's by a relative error of at most 0.0065.
Values may be sent and summed in bfloat16 or wider, within the bound.
A program may use at most 128 MiB of HBM per device.

```python
import math
import jax
import jax.numpy as jnp
import numpy as np
from jax import lax

HD = 128
QH = 24
KVH = 4
GROUP = 6
D = 3072
EXPERTS = 8
TOP = 2
FF = 1024
MB_ROWS = 4
CAP = 2
SEQS = 128
L = 128


def draw_query(key, part):
    key = jax.random.fold_in(key, 11)
    key_one = jax.random.fold_in(key, 0)
    values = jnp.clip(jax.random.normal(key_one, (SEQS, QH * HD), jnp.float32), -6.0, 6.0)
    return values.astype(jnp.bfloat16)


def draw_key_cache(key, part):
    key = jax.random.fold_in(key, 12)
    values = jnp.clip(jax.random.normal(key, (SEQS, L, KVH * HD), jnp.float32), -6.0, 6.0)
    return values.astype(jnp.bfloat16)


def draw_lengths(key, part):
    key = jax.random.fold_in(key, 13)
    key_one, key_two = jax.random.split(key)
    drawn = jax.random.randint(key_one, (SEQS,), 2, L + 1)
    picked = jax.random.randint(key_two, (), 0, SEQS)
    return jnp.where(jnp.arange(SEQS, dtype=jnp.int32) == picked, L, drawn).astype(jnp.int32)


def block_scale(rng, dims, shards, low, top_value):
    def one(position, blocks):
        heights = jax.random.uniform(jax.random.fold_in(jax.random.fold_in(rng, 6), position), (blocks,), jnp.float32, low / len(shards), top_value / len(shards))
        return jnp.repeat(jnp.exp(heights), dims[position] // blocks).reshape((-1,) + (1,) * (len(dims) - position - 1))

    loudness = one(*shards[0])
    for cut in shards[1:]:
        loudness = loudness * one(*cut)
    return loudness


def routed_block(rng, own, number, rows, amount, top, most, slope):
    ranking = jax.random.permutation(rng, amount)
    heavy_load, common = load_shares(amount, rows * top, most, slope, True), load_shares(amount, rows * top, most, slope, False)
    places = jnp.arange(amount)

    def named(sizes, rotation):
        used = int((sizes > 0).sum())
        fixed = max(1, used // 4)
        shifted = fixed + (places - fixed + rotation * (used - fixed)) % max(1, amount - fixed)
        return jnp.zeros((amount,), jnp.int32).at[ranking[jnp.where(places < fixed, places, shifted)]].set(jnp.asarray(sizes, jnp.int32))

    sizes = jnp.where(number % 4 == 0, named(heavy_load, number // 4), named(common, number - number // 4 - 1))
    mixed = jax.random.permutation(jax.random.fold_in(own, 3), amount)
    giver, taker = mixed[0:amount // 2 * 2:2], mixed[1:amount // 2 * 2:2]
    room = jnp.minimum(sizes[giver] - 1, most - sizes[taker]) // 2
    room = jnp.where((giver == ranking[0]) | (taker == ranking[0]) | (sizes[taker] == 0), 0, jnp.maximum(room, 0))
    shifted = jax.random.randint(jax.random.fold_in(own, 4), (amount // 2,), 0, 1 << 20) % (room + 1)
    sizes = sizes.at[giver].add(-shifted).at[taker].add(shifted)
    items = jnp.searchsorted(jnp.cumsum(sizes), jnp.arange(rows * top), side="right").astype(jnp.int32)
    grid = items.reshape(top, rows).T
    grid = grid[jax.random.permutation(jax.random.fold_in(own, 1), rows)]
    rotation = jax.random.randint(jax.random.fold_in(own, 2), (rows, 1), 0, top)
    return jnp.take_along_axis(grid, (jnp.arange(top)[None, :] + rotation) % top, axis=1)


def load_shares(number_of, total, most, skew, full):
    portions = [(1 << 20) // math.isqrt(grade ** skew) + 1 for grade in range(1, number_of + 1)]
    largest = most if full else min(most, max(-(-total // number_of), total * portions[0] // sum(portions)))
    least = 1 if total - largest >= number_of - 1 else 0
    given, surplus = [largest] + [least] * (number_of - 1), total - largest - least * (number_of - 1)
    while surplus > 0:
        free = [i for i in range(1, number_of) if given[i] < largest] or [i for i in range(1, number_of) if given[i] < most]
        mass, budget = sum([portions[i] for i in free]), surplus
        for i in free:
            more = min(most - given[i], max(1, budget * portions[i] // mass), surplus)
            given[i] = given[i] + more
            surplus = surplus - more
    return np.array(given)


def centred(rng, shape, scale, most, shards=(), held_as=jnp.bfloat16):
    loudness = block_scale(rng, shape, shards, -0.22, 0.18) if shards else 1.0
    values = jax.random.normal(rng, shape, jnp.float32) * scale * loudness
    return jnp.minimum(jnp.maximum(values, -most), most).astype(held_as)


def setup_inputs(seed: int = 0, part: int = 0) -> dict:
    key_list = jax.random.split(jax.random.key(seed), 14)
    part_splits = jax.random.split(jax.random.fold_in(key_list[13], part), 14)
    query = draw_query(jax.random.fold_in(jax.random.fold_in(key_list[13], part), 71), part)
    new_key = centred(part_splits[1], (SEQS, KVH * HD), 1.0, 6.0, ((0, 16),))
    new_value = centred(part_splits[2], (SEQS, KVH * HD), 1.0, 6.0, ((0, 16),))
    key_cache = draw_key_cache(jax.random.fold_in(jax.random.fold_in(key_list[13], part), 71), part)
    value_cache = centred(part_splits[4], (SEQS, L, KVH * HD), 1.0, 6.0, ((0, 16),))
    lengths = draw_lengths(jax.random.fold_in(jax.random.fold_in(key_list[13], part), 71), part)
    residual = centred(part_splits[6], (SEQS, D), 1.0, 6.0, ((0, 16),))
    norm_gain = jnp.clip(1.0 + 0.12 * jax.random.normal(key_list[7], (D,), jnp.float32), 0.3984375, 1.59375).astype(jnp.bfloat16)
    router = centred(key_list[8], (D, EXPERTS), D ** -0.5, 0.109375)
    routes_keys = jax.random.split(jax.random.fold_in(part_splits[9], 1), SEQS // MB_ROWS)
    routes_turns = jax.random.permutation(jax.random.fold_in(part_splits[9], 3), SEQS // MB_ROWS)
    routes = jax.vmap(lambda own, number: routed_block(jax.random.fold_in(part_splits[9], 2), own, number, MB_ROWS, EXPERTS, TOP, CAP, 2))(routes_keys, routes_turns).reshape((SEQS, TOP))
    w_gate = centred(key_list[10], (D, EXPERTS * FF), D ** -0.5, 0.109375, ((1, 16),))
    w_up = centred(key_list[11], (D, EXPERTS * FF), D ** -0.5, 0.109375, ((1, 16),))
    w_down = centred(key_list[12], (EXPERTS * FF, D), FF ** -0.5, 0.1875, ((0, 16),))
    return {"query": query, "new_key": new_key, "new_value": new_value, "key_cache": key_cache, "value_cache": value_cache, "lengths": lengths, "residual": residual, "norm_gain": norm_gain, "router": router, "routes": routes, "w_gate": w_gate, "w_up": w_up, "w_down": w_down}


def reference(query, new_key, new_value, key_cache, value_cache, lengths, residual, norm_gain, router, routes, w_gate, w_up, w_down):
    seq_count = query.shape[0]
    scale = HD ** (-0.5)
    q_heads = query.astype(jnp.float32).reshape(seq_count, KVH, GROUP, HD)
    keys = key_cache.astype(jnp.float32).reshape(seq_count, L, KVH, HD)
    values = value_cache.astype(jnp.float32).reshape(seq_count, L, KVH, HD)
    own_key = new_key.astype(jnp.float32).reshape(seq_count, KVH, HD)
    own_value = new_value.astype(jnp.float32).reshape(seq_count, KVH, HD)
    scores = jnp.einsum('sjgd,sljd->sjgl', q_heads, keys) * scale
    own_score = jnp.einsum('sjgd,sjd->sjg', q_heads, own_key) * scale
    live = jnp.arange(L, dtype=jnp.int32)[None, :] < lengths[:, None]
    scores = jnp.where(live[:, None, None, :], scores, -jnp.inf)
    top_score = jnp.maximum(lax.optimization_barrier(jnp.max(scores, axis=-1)), own_score)
    weights = jnp.exp(scores - top_score[..., None])
    own_weight = jnp.exp(own_score - top_score)
    total = lax.optimization_barrier(jnp.sum(weights, axis=-1)) + own_weight
    weights_low = lax.optimization_barrier(weights.astype(jnp.bfloat16)).astype(jnp.float32)
    own_low = lax.optimization_barrier(own_weight.astype(jnp.bfloat16)).astype(jnp.float32)
    mixed = jnp.einsum('sjgl,sljd->sjgd', weights_low, values) + own_low[..., None] * own_value[:, :, None, :]
    attention = (mixed / total[..., None]).reshape(seq_count, QH * HD)
    mid = (residual.astype(jnp.float32) + attention).astype(jnp.bfloat16)
    mid_f = mid.astype(jnp.float32)
    normed = (mid_f * lax.rsqrt(lax.optimization_barrier(jnp.mean(mid_f * mid_f, axis=-1, keepdims=True)) + 1e-05) * norm_gain.astype(jnp.float32)).astype(jnp.bfloat16)
    logits = jnp.dot(normed, router, preferred_element_type=jnp.float32)
    onehot = (routes[:, :, None] == jnp.arange(EXPERTS, dtype=jnp.int32)[None, None, :]).astype(jnp.float32)
    chosen = lax.optimization_barrier(jnp.sum(onehot * logits[:, None, :], axis=-1))
    first = jax.nn.sigmoid(chosen[:, 0] - chosen[:, 1])
    second = jax.nn.sigmoid(chosen[:, 1] - chosen[:, 0])
    gates = (first[:, None] * onehot[:, 0] + second[:, None] * onehot[:, 1]).astype(jnp.bfloat16)
    routed = lax.optimization_barrier(jnp.sum(onehot, axis=1))
    bound = seq_count // MB_ROWS * CAP
    moe = jnp.zeros((seq_count, D), jnp.float32)
    for expert in range(EXPERTS):
        picked = jnp.nonzero(routed[:, expert] > 0, size=bound, fill_value=0)[0].astype(jnp.int32)
        valid = (jnp.arange(bound, dtype=jnp.int32) < jnp.sum(routed[:, expert] > 0).astype(jnp.int32)).astype(jnp.float32)
        rows = normed[picked]
        gate_part = jnp.dot(rows, w_gate[:, expert * FF:(expert + 1) * FF], preferred_element_type=jnp.float32)
        up_part = jnp.dot(rows, w_up[:, expert * FF:(expert + 1) * FF], preferred_element_type=jnp.float32)
        hidden = (jax.nn.silu(gate_part) * up_part).astype(jnp.bfloat16)
        expert_out = jnp.dot(hidden, w_down[expert * FF:(expert + 1) * FF], preferred_element_type=jnp.float32)
        weight_rows = valid * gates[picked, expert].astype(jnp.float32)
        moe = moe.at[picked].add(weight_rows[:, None] * expert_out)
    return (mid_f + moe).astype(jnp.bfloat16)
```

```python
import functools

import jax
import jax.numpy as jnp
from jax import lax
from jax.experimental import pallas as pl
from jax.experimental.pallas import tpu as pltpu
from jax.sharding import PartitionSpec as P

HD = 128
TILE = 16
F32 = jnp.float32
BF16 = jnp.bfloat16
MESH = pl.DeviceIdType.MESH


def dot(a, b):
    return jnp.dot(a, b, preferred_element_type=F32)


def iota(shape, dim):
    return lax.broadcasted_iota(jnp.int32, shape, dim)


def attend(query_ref, new_key_ref, new_value_ref, lengths_ref, keys, values, values_ready, q_rows, o_rows):
    seqs, width = query_ref.shape
    kv = new_key_ref.shape[1]
    heads = width // HD
    group = width // kv
    slots = keys.shape[1]
    scale = HD ** (-0.5)
    query = query_ref[...].astype(F32)
    for h in range(heads):
        q_rows[pl.ds(h, seqs, stride=heads), :] = query[:, h * HD : (h + 1) * HD]
    own_keys = new_key_ref[...].astype(F32)
    own_values = new_value_ref[...].astype(F32)
    mine = iota((heads, kv), 0) // group == iota((heads, kv), 1) // HD
    position = iota((heads, slots), 1)
    scores, own = [], []
    for s in range(seqs):
        q = q_rows[s * heads : (s + 1) * heads, :]
        wide = jnp.where(mine, jnp.concatenate([q] * (kv // HD), axis=1), 0.0)
        score = lax.dot_general(
            wide.astype(BF16), keys[s], (((1,), (1,)), ((), ())), preferred_element_type=F32
        )
        scores.append(jnp.where(position < lengths_ref[s], score * scale, -jnp.inf))
        own.append(jnp.sum(wide * own_keys[s : s + 1, :], axis=1, keepdims=True) * scale)
    values_ready()
    for s in range(seqs):
        top = jnp.maximum(jnp.max(scores[s], axis=1, keepdims=True), own[s])
        weights = jnp.exp(scores[s] - top)
        own_weight = jnp.exp(own[s] - top)
        total = jnp.sum(weights, axis=1, keepdims=True) + own_weight
        mixed = dot(weights.astype(BF16), values[s])
        mixed = mixed + own_weight.astype(BF16).astype(F32) * own_values[s : s + 1, :]
        mixed = jnp.where(mine, mixed, 0.0)
        summed = mixed[:, :HD]
        for j in range(1, kv // HD):
            summed = summed + mixed[:, j * HD : (j + 1) * HD]
        o_rows[s * heads : (s + 1) * heads, :] = summed / total
    return jnp.concatenate(
        [o_rows[pl.ds(h, seqs, stride=heads), :] for h in range(heads)], axis=1
    )


def kernel(
    side,
    query_ref,
    new_key_ref,
    new_value_ref,
    lengths_ref,
    residual_ref,
    gain_ref,
    router_ref,
    routes_ref,
    key_hbm,
    value_hbm,
    gate_hbm,
    up_hbm,
    down_hbm,
    out_ref,
    keys,
    values,
    w_gate,
    w_up,
    w_down,
    q_rows,
    o_rows,
    packed,
    arrived,
    hidden,
    partial,
    part_out,
    part_in,
    back_out,
    back_in,
    load_sem,
    send_sem,
    recv_sem,
    fsend_sem,
    frecv_sem,
    psend_sem,
    precv_sem,
    rsend_sem,
    rrecv_sem,
):
    seqs, width = residual_ref.shape
    experts = router_ref.shape[0]
    members = side // experts
    cap = seqs // 2
    cuts = TILE // cap
    piece = width // cuts
    rows = experts * TILE
    each = experts * cap
    me = lax.axis_index("side")
    chip = me // members
    lane = lax.rem(me, members)

    loads = []
    for n, (src, dst) in enumerate(
        (
            (key_hbm, keys),
            (value_hbm, values),
            (gate_hbm, w_gate),
            (up_hbm, w_up),
            (down_hbm, w_down),
        )
    ):
        load = pltpu.make_async_copy(src, dst, load_sem.at[n])
        load.start()
        loads.append(load)

    others = [lax.rem(chip + d, experts) for d in range(1, experts)]
    mates = [lax.rem(lane + j, members) for j in range(1, members)]
    barrier = pltpu.get_barrier_semaphore()
    for other in others:
        pl.semaphore_signal(
            barrier, inc=1, device_id={"side": other * members + lane}, device_id_type=MESH
        )
    for mate in mates:
        pl.semaphore_signal(
            barrier, inc=1, device_id={"side": chip * members + mate}, device_id_type=MESH
        )

    ids = iota((seqs, experts), 1)
    first_hot = (routes_ref[:, 0:1] == ids).astype(F32)
    second_hot = (routes_ref[:, 1:2] == ids).astype(F32)
    routed = (first_hot + second_hot).astype(BF16)
    earlier = (iota((seqs, seqs), 0) > iota((seqs, seqs), 1)).astype(BF16)
    rank = dot(earlier, routed).astype(BF16)
    spread = (iota((experts, rows), 0) == iota((experts, rows), 1) // TILE).astype(BF16)
    slot = lax.rem(iota((seqs, rows), 1), cap).astype(F32)
    chosen = jnp.where(dot(rank, spread) == slot, dot(routed, spread), 0.0)
    cut_mask = iota((cuts * seqs, rows), 0) // seqs == lax.rem(
        iota((cuts * seqs, rows), 1) // cap, cuts
    )
    select = jnp.where(cut_mask, jnp.concatenate([chosen] * cuts, axis=0), 0.0)

    loads[0].wait()
    attention = attend(
        query_ref, new_key_ref, new_value_ref, lengths_ref, keys, values, loads[1].wait, q_rows, o_rows
    )
    mid = (residual_ref[...].astype(F32) + attention).astype(BF16).astype(F32)
    normed = (
        mid
        * lax.rsqrt(jnp.mean(mid * mid, axis=1, keepdims=True) + 1e-05)
        * gain_ref[...].astype(F32)
    )
    stacked = jnp.concatenate(
        [normed[:, b * piece : (b + 1) * piece] for b in range(cuts)], axis=0
    ).astype(BF16)
    packed[...] = (
        dot(select.T.astype(BF16), stacked).astype(BF16).reshape(experts, TILE, piece)
    )

    pl.semaphore_wait(barrier, len(others) + len(mates))
    sends = []
    for d, other in enumerate(others):
        copy = pltpu.make_async_remote_copy(
            src_ref=packed.at[other],
            dst_ref=arrived.at[lane, chip],
            send_sem=send_sem.at[d],
            recv_sem=recv_sem.at[chip],
            device_id={"side": other * members + lane},
            device_id_type=MESH,
        )
        copy.start()
        sends.append(copy)
    arrived[lane, chip] = packed[chip]

    def forward(d, source):
        for j, mate in enumerate(mates):
            copy = pltpu.make_async_remote_copy(
                src_ref=arrived.at[lane, source],
                dst_ref=arrived.at[lane, source],
                send_sem=fsend_sem.at[j, d],
                recv_sem=frecv_sem.at[lane, source],
                device_id={"side": chip * members + mate},
                device_id_type=MESH,
            )
            copy.start()
            sends.append(copy)

    forward(0, chip)

    logits = lax.dot_general(
        normed.astype(BF16), router_ref[...], (((1,), (1,)), ((), ())), preferred_element_type=F32
    )
    gap = jnp.sum((first_hot - second_hot) * logits, axis=1, keepdims=True)
    gates = first_hot * jax.nn.sigmoid(gap) + second_hot * jax.nn.sigmoid(-gap)
    combine = (
        jnp.where(cut_mask, jnp.concatenate([dot(gates.astype(BF16), spread)] * cuts, axis=0), 0.0)
        * select
    ).astype(BF16)

    r, q = iota((rows, rows), 0), iota((rows, rows), 1)
    order = (
        lax.rem(r, each) // cap * TILE + r // each * cap + lax.rem(r, cap) == q
    ).astype(BF16)

    def sources():
        return [(d, lax.rem(chip + experts - d, experts)) for d in range(1, experts)]

    for d, source in sources():
        pltpu.make_async_remote_copy(
            src_ref=packed.at[source],
            dst_ref=arrived.at[lane, source],
            send_sem=send_sem.at[d - 1],
            recv_sem=recv_sem.at[source],
            device_id={"side": source * members + lane},
            device_id_type=MESH,
        ).wait_recv()
        forward(d, source)
    for load in loads[2:]:
        load.wait()
    for d, source in [(0, chip)] + sources():
        for j, mate in enumerate(mates):
            pltpu.make_async_remote_copy(
                src_ref=arrived.at[mate, source],
                dst_ref=arrived.at[mate, source],
                send_sem=fsend_sem.at[j, d],
                recv_sem=frecv_sem.at[mate, source],
                device_id={"side": chip * members + mate},
                device_id_type=MESH,
            ).wait_recv()

    def give(b):
        for j, mate in enumerate(mates):
            copy = pltpu.make_async_remote_copy(
                src_ref=part_out.at[mate, b],
                dst_ref=part_in.at[lane, b],
                send_sem=psend_sem.at[j, b],
                recv_sem=precv_sem.at[lane, b],
                device_id={"side": chip * members + mate},
                device_id_type=MESH,
            )
            copy.start()
            sends.append(copy)

    pair = min(2, members)
    blocks = members // pair

    def expand(block):
        tokens = [
            dot(order, arrived[block * pair + n].reshape(rows, piece)).astype(BF16)
            for n in range(pair)
        ]
        gate_part = up_part = 0.0
        for b in range(cuts):
            x = jnp.concatenate([t[b * each : (b + 1) * each] for t in tokens], axis=0)
            gate_part = gate_part + dot(x, w_gate[b * piece : (b + 1) * piece, :])
            up_part = up_part + dot(x, w_up[b * piece : (b + 1) * piece, :])
        hidden[block] = (jax.nn.silu(gate_part) * up_part).astype(BF16)

    def contract(block, b):
        y = dot(hidden[block], w_down[:, b * piece : (b + 1) * piece]).reshape(pair, each, piece)
        for n in range(pair):
            partial[block * pair + n, b] = y[n]
            part_out[block * pair + n, b] = y[n].astype(BF16)

    def over(fn):
        if blocks == 1:
            fn(0)
        else:
            pl.loop(0, blocks)(fn)

    over(expand)
    for b in range(cuts):
        over(functools.partial(contract, b=b))
        give(b)

    sums = []
    for b in range(cuts):
        total = partial[lane, b]
        for j, mate in enumerate(mates):
            pltpu.make_async_remote_copy(
                src_ref=part_out.at[mate, b],
                dst_ref=part_in.at[mate, b],
                send_sem=psend_sem.at[j, b],
                recv_sem=precv_sem.at[mate, b],
                device_id={"side": chip * members + mate},
                device_id_type=MESH,
            ).wait_recv()
            total = total + part_in[mate, b].astype(F32)
        sums.append(total.astype(BF16))
    order_back = (
        lax.rem(q, each) // cap * TILE + q // each * cap + lax.rem(q, cap) == r
    ).astype(BF16)
    back_out[...] = (
        dot(order_back, jnp.concatenate(sums, axis=0)).astype(BF16).reshape(experts, TILE, piece)
    )
    for d, other in enumerate(others):
        copy = pltpu.make_async_remote_copy(
            src_ref=back_out.at[other],
            dst_ref=back_in.at[chip],
            send_sem=rsend_sem.at[d],
            recv_sem=rrecv_sem.at[chip],
            device_id={"side": other * members + lane},
            device_id_type=MESH,
        )
        copy.start()
        sends.append(copy)
    back_in[chip] = back_out[chip]
    for d, source in sources():
        pltpu.make_async_remote_copy(
            src_ref=back_out.at[source],
            dst_ref=back_in.at[source],
            send_sem=rsend_sem.at[d - 1],
            recv_sem=rrecv_sem.at[source],
            device_id={"side": source * members + lane},
            device_id_type=MESH,
        ).wait_recv()
    moe = dot(combine, back_in[...].reshape(rows, piece))
    for b in range(cuts):
        columns = slice(b * piece, (b + 1) * piece)
        out_ref[:, columns] = (mid[:, columns] + moe[b * seqs : (b + 1) * seqs]).astype(BF16)
    for copy in sends:
        copy.wait_send()


def on_device(
    query,
    new_key,
    new_value,
    key_cache,
    value_cache,
    lengths,
    residual,
    norm_gain,
    router,
    routes,
    w_gate,
    w_up,
    w_down,
):
    seqs, width = residual.shape
    experts = router.shape[1]
    side = lax.axis_size("side")
    members = side // experts
    cap = seqs // 2
    cuts = TILE // cap
    piece = width // cuts
    each = experts * cap
    pair = min(2, members)
    heads = width // HD
    vmem = pl.BlockSpec(memory_space=pltpu.VMEM)
    hbm = pl.BlockSpec(memory_space=pl.ANY)
    dma = pltpu.SemaphoreType.DMA
    return pl.pallas_call(
        functools.partial(kernel, side),
        out_shape=jax.ShapeDtypeStruct((seqs, width), BF16),
        in_specs=[vmem, vmem, vmem, pl.BlockSpec(memory_space=pltpu.SMEM)] + [vmem] * 4 + [hbm] * 5,
        out_specs=vmem,
        scratch_shapes=[
            pltpu.VMEM(key_cache.shape, BF16),
            pltpu.VMEM(value_cache.shape, BF16),
            pltpu.VMEM(w_gate.shape, BF16),
            pltpu.VMEM(w_up.shape, BF16),
            pltpu.VMEM(w_down.shape, BF16),
            pltpu.VMEM((seqs * heads, HD), F32),
            pltpu.VMEM((seqs * heads, HD), F32),
            pltpu.VMEM((experts, TILE, piece), BF16),
            pltpu.VMEM((members, experts, TILE, piece), BF16),
            pltpu.VMEM((members // pair, pair * each, w_gate.shape[1]), BF16),
            pltpu.VMEM((members, cuts, each, piece), F32),
            pltpu.VMEM((members, cuts, each, piece), BF16),
            pltpu.VMEM((members, cuts, each, piece), BF16),
            pltpu.VMEM((experts, TILE, piece), BF16),
            pltpu.VMEM((experts, TILE, piece), BF16),
            dma((5,)),
            dma((experts - 1,)),
            dma((experts,)),
            dma((members, experts)),
            dma((members, experts)),
            dma((members, cuts)),
            dma((members, cuts)),
            dma((experts - 1,)),
            dma((experts,)),
        ],
        compiler_params=pltpu.CompilerParams(
            collective_id=0, has_side_effects=True, vmem_limit_bytes=50 * 1024 * 1024
        ),
    )(
        query,
        new_key,
        new_value,
        lengths,
        residual,
        norm_gain[None, :],
        router.T,
        routes,
        key_cache,
        value_cache,
        w_gate,
        w_up,
        w_down,
    )


def solution(mesh):
    in_specs = (
        P(("groups", "side"), None),
        P(("groups", "side"), None),
        P(("groups", "side"), None),
        P(("groups", "side"), None, None),
        P(("groups", "side"), None, None),
        P(("groups", "side")),
        P(("groups", "side"), None),
        P(),
        P(),
        P(("groups", "side"), None),
        P(None, "side"),
        P(None, "side"),
        P("side", None),
    )
    out_specs = P(("groups", "side"), None)
    return jax.shard_map(
        on_device, mesh=mesh, in_specs=in_specs, out_specs=out_specs, check_vma=False
    )
```

```python
import functools

import jax
import jax.numpy as jnp
from jax import lax
from jax.experimental import pallas as pl
from jax.experimental.pallas import tpu as pltpu
from jax.sharding import PartitionSpec as P

HD = 128
TILE = 16
F32 = jnp.float32
BF16 = jnp.bfloat16
MESH = pl.DeviceIdType.MESH


def dot(a, b):
    return jnp.dot(a, b, preferred_element_type=F32)


def iota(shape, dim):
    return lax.broadcasted_iota(jnp.int32, shape, dim)


def attend(query_ref, new_key_ref, new_value_ref, lengths_ref, keys, values, values_ready, q_rows, o_rows):
    seqs, width = query_ref.shape
    kv = new_key_ref.shape[1]
    heads = width // HD
    group = width // kv
    slots = keys.shape[1]
    scale = HD ** (-0.5)
    query = query_ref[...].astype(F32)
    for h in range(heads):
        q_rows[pl.ds(h, seqs, stride=heads), :] = query[:, h * HD : (h + 1) * HD]
    own_keys = new_key_ref[...].astype(F32)
    mine = iota((heads, kv), 0) // group == iota((heads, kv), 1) // HD
    position = iota((heads, slots), 1)
    scores, own = [], []
    for s in range(seqs):
        q = q_rows[s * heads : (s + 1) * heads, :]
        wide = jnp.where(mine, jnp.concatenate([q] * (kv // HD), axis=1), 0.0)
        score = lax.dot_general(
            wide.astype(BF16), keys[s], (((1,), (1,)), ((), ())), preferred_element_type=F32
        )
        scores.append(jnp.where(position < lengths_ref[s], score * scale, -jnp.inf))
        own.append(jnp.sum(wide * own_keys[s : s + 1, :], axis=1, keepdims=True) * scale)
    values_ready()
    own_values = new_value_ref[...].astype(F32)
    for s in range(seqs):
        top = jnp.maximum(jnp.max(scores[s], axis=1, keepdims=True), own[s])
        weights = jnp.exp(scores[s] - top)
        own_weight = jnp.exp(own[s] - top)
        total = jnp.sum(weights, axis=1, keepdims=True) + own_weight
        mixed = dot(weights.astype(BF16), values[s])
        mixed = mixed + own_weight.astype(BF16).astype(F32) * own_values[s : s + 1, :]
        mixed = jnp.where(mine, mixed, 0.0)
        summed = mixed[:, :HD]
        for j in range(1, kv // HD):
            summed = summed + mixed[:, j * HD : (j + 1) * HD]
        o_rows[s * heads : (s + 1) * heads, :] = summed / total
    return jnp.concatenate(
        [o_rows[pl.ds(h, seqs, stride=heads), :] for h in range(heads)], axis=1
    )


def kernel(
    side,
    query_hbm,
    new_key_hbm,
    new_value_hbm,
    lengths_hbm,
    residual_hbm,
    gain_hbm,
    router_hbm,
    routes_hbm,
    key_hbm,
    value_hbm,
    gate_hbm,
    up_hbm,
    down_hbm,
    out_ref,
    query_ref,
    new_key_ref,
    new_value_ref,
    lengths_ref,
    residual_ref,
    gain_ref,
    router_ref,
    routes_ref,
    keys,
    values,
    w_gate,
    w_up,
    w_down,
    q_rows,
    o_rows,
    packed,
    arrived,
    hidden,
    partial,
    part_out,
    part_in,
    back_out,
    back_in,
    load_sem,
    send_sem,
    recv_sem,
    fsend_sem,
    frecv_sem,
    psend_sem,
    precv_sem,
    rsend_sem,
    rrecv_sem,
):
    seqs, width = residual_hbm.shape
    experts = router_hbm.shape[0]
    members = side // experts
    cap = seqs // 2
    cuts = TILE // cap
    piece = width // cuts
    rows = experts * TILE
    each = experts * cap
    me = lax.axis_index("side")
    chip = me // members
    lane = lax.rem(me, members)

    loads = []
    for n, (src, dst) in enumerate(
        (
            (routes_hbm, routes_ref),
            (query_hbm, query_ref),
            (lengths_hbm, lengths_ref),
            (new_key_hbm, new_key_ref),
            (key_hbm, keys),
            (new_value_hbm, new_value_ref),
            (value_hbm, values),
            (residual_hbm, residual_ref),
            (gain_hbm, gain_ref),
            (router_hbm, router_ref),
            (gate_hbm, w_gate),
            (up_hbm, w_up),
            (down_hbm, w_down),
        )
    ):
        load = pltpu.make_async_copy(src, dst, load_sem.at[n])
        load.start()
        loads.append(load)

    others = [lax.rem(chip + d, experts) for d in range(1, experts)]
    mates = [lax.rem(lane + j, members) for j in range(1, members)]
    barrier = pltpu.get_barrier_semaphore()
    for other in others:
        pl.semaphore_signal(
            barrier, inc=1, device_id={"side": other * members + lane}, device_id_type=MESH
        )
    for mate in mates:
        pl.semaphore_signal(
            barrier, inc=1, device_id={"side": chip * members + mate}, device_id_type=MESH
        )

    ids = iota((seqs, experts), 1)
    loads[0].wait()
    diagonal = iota((seqs, seqs), 0) == iota((seqs, seqs), 1)
    first_hot, second_hot = [
        (
            jnp.sum(jnp.where(diagonal, routes_ref[n : n + 1, :], 0), axis=1, keepdims=True) == ids
        ).astype(F32)
        for n in range(2)
    ]
    routed = (first_hot + second_hot).astype(BF16)
    earlier = (iota((seqs, seqs), 0) > iota((seqs, seqs), 1)).astype(BF16)
    rank = dot(earlier, routed).astype(BF16)
    spread = (iota((experts, rows), 0) == iota((experts, rows), 1) // TILE).astype(BF16)
    slot = lax.rem(iota((seqs, rows), 1), cap).astype(F32)
    chosen = jnp.where(dot(rank, spread) == slot, dot(routed, spread), 0.0)
    cut_mask = iota((cuts * seqs, rows), 0) // seqs == lax.rem(
        iota((cuts * seqs, rows), 1) // cap, cuts
    )
    select = jnp.where(cut_mask, jnp.concatenate([chosen] * cuts, axis=0), 0.0)

    for load in loads[1:5]:
        load.wait()

    def values_ready():
        for load in loads[5:10]:
            load.wait()

    attention = attend(
        query_ref, new_key_ref, new_value_ref, lengths_ref, keys, values, values_ready, q_rows, o_rows
    )
    mid = (residual_ref[...].astype(F32) + attention).astype(BF16).astype(F32)
    normed = (
        mid
        * lax.rsqrt(jnp.mean(mid * mid, axis=1, keepdims=True) + 1e-05)
        * gain_ref[...].astype(F32).reshape(1, width)
    )
    stacked = jnp.concatenate(
        [normed[:, b * piece : (b + 1) * piece] for b in range(cuts)], axis=0
    ).astype(BF16)
    packed[...] = (
        dot(select.T.astype(BF16), stacked).astype(BF16).reshape(experts, TILE, piece)
    )

    pl.semaphore_wait(barrier, len(others) + len(mates))
    sends = []
    for d, other in enumerate(others):
        copy = pltpu.make_async_remote_copy(
            src_ref=packed.at[other],
            dst_ref=arrived.at[lane, chip],
            send_sem=send_sem.at[d],
            recv_sem=recv_sem.at[chip],
            device_id={"side": other * members + lane},
            device_id_type=MESH,
        )
        copy.start()
        sends.append(copy)
    arrived[lane, chip] = packed[chip]

    def forward(d, source):
        for j, mate in enumerate(mates):
            copy = pltpu.make_async_remote_copy(
                src_ref=arrived.at[lane, source],
                dst_ref=arrived.at[lane, source],
                send_sem=fsend_sem.at[j, d],
                recv_sem=frecv_sem.at[lane, source],
                device_id={"side": chip * members + mate},
                device_id_type=MESH,
            )
            copy.start()
            sends.append(copy)

    forward(0, chip)

    logits = lax.dot_general(
        normed.astype(BF16), router_ref[...], (((1,), (1,)), ((), ())), preferred_element_type=F32
    )
    gap = jnp.sum((first_hot - second_hot) * logits, axis=1, keepdims=True)
    gates = first_hot * jax.nn.sigmoid(gap) + second_hot * jax.nn.sigmoid(-gap)
    combine = (
        jnp.where(cut_mask, jnp.concatenate([dot(gates.astype(BF16), spread)] * cuts, axis=0), 0.0)
        * select
    ).astype(BF16)

    r, q = iota((rows, rows), 0), iota((rows, rows), 1)
    order = (
        lax.rem(r, each) // cap * TILE + r // each * cap + lax.rem(r, cap) == q
    ).astype(BF16)

    def sources():
        return [(d, lax.rem(chip + experts - d, experts)) for d in range(1, experts)]

    for d, source in sources():
        pltpu.make_async_remote_copy(
            src_ref=packed.at[source],
            dst_ref=arrived.at[lane, source],
            send_sem=send_sem.at[d - 1],
            recv_sem=recv_sem.at[source],
            device_id={"side": source * members + lane},
            device_id_type=MESH,
        ).wait_recv()
        forward(d, source)
    for load in loads[10:]:
        load.wait()
    for d, source in [(0, chip)] + sources():
        for j, mate in enumerate(mates):
            pltpu.make_async_remote_copy(
                src_ref=arrived.at[mate, source],
                dst_ref=arrived.at[mate, source],
                send_sem=fsend_sem.at[j, d],
                recv_sem=frecv_sem.at[mate, source],
                device_id={"side": chip * members + mate},
                device_id_type=MESH,
            ).wait_recv()

    def give(b):
        for j, mate in enumerate(mates):
            copy = pltpu.make_async_remote_copy(
                src_ref=part_out.at[mate, b],
                dst_ref=part_in.at[lane, b],
                send_sem=psend_sem.at[j, b],
                recv_sem=precv_sem.at[lane, b],
                device_id={"side": chip * members + mate},
                device_id_type=MESH,
            )
            copy.start()
            sends.append(copy)

    pair = min(2, members)
    blocks = members // pair

    def expand(block):
        tokens = [
            dot(order, arrived[block * pair + n].reshape(rows, piece)).astype(BF16)
            for n in range(pair)
        ]
        gate_part = up_part = 0.0
        for b in range(cuts):
            x = jnp.concatenate([t[b * each : (b + 1) * each] for t in tokens], axis=0)
            gate_part = gate_part + dot(x, w_gate[b * piece : (b + 1) * piece, :])
            up_part = up_part + dot(x, w_up[b * piece : (b + 1) * piece, :])
        hidden[block] = (jax.nn.silu(gate_part) * up_part).astype(BF16)

    def contract(block, b):
        y = dot(hidden[block], w_down[:, b * piece : (b + 1) * piece]).reshape(pair, each, piece)
        for n in range(pair):
            partial[block * pair + n, b] = y[n]
            part_out[block * pair + n, b] = y[n].astype(BF16)

    def over(fn):
        if blocks == 1:
            fn(0)
        else:
            pl.loop(0, blocks)(fn)

    over(expand)
    for b in range(cuts):
        over(functools.partial(contract, b=b))
        give(b)

    sums = []
    for b in range(cuts):
        total = partial[lane, b]
        for j, mate in enumerate(mates):
            pltpu.make_async_remote_copy(
                src_ref=part_out.at[mate, b],
                dst_ref=part_in.at[mate, b],
                send_sem=psend_sem.at[j, b],
                recv_sem=precv_sem.at[mate, b],
                device_id={"side": chip * members + mate},
                device_id_type=MESH,
            ).wait_recv()
            total = total + part_in[mate, b].astype(F32)
        sums.append(total.astype(BF16))
    order_back = (
        lax.rem(q, each) // cap * TILE + q // each * cap + lax.rem(q, cap) == r
    ).astype(BF16)
    back_out[...] = (
        dot(order_back, jnp.concatenate(sums, axis=0)).astype(BF16).reshape(experts, TILE, piece)
    )
    for d, other in enumerate(others):
        copy = pltpu.make_async_remote_copy(
            src_ref=back_out.at[other],
            dst_ref=back_in.at[chip],
            send_sem=rsend_sem.at[d],
            recv_sem=rrecv_sem.at[chip],
            device_id={"side": other * members + lane},
            device_id_type=MESH,
        )
        copy.start()
        sends.append(copy)
    back_in[chip] = back_out[chip]
    for d, source in sources():
        pltpu.make_async_remote_copy(
            src_ref=back_out.at[source],
            dst_ref=back_in.at[source],
            send_sem=rsend_sem.at[d - 1],
            recv_sem=rrecv_sem.at[source],
            device_id={"side": source * members + lane},
            device_id_type=MESH,
        ).wait_recv()
    moe = dot(combine, back_in[...].reshape(rows, piece))
    for b in range(cuts):
        columns = slice(b * piece, (b + 1) * piece)
        out_ref[:, columns] = (mid[:, columns] + moe[b * seqs : (b + 1) * seqs]).astype(BF16)
    for copy in sends:
        copy.wait_send()


def on_device(
    query,
    new_key,
    new_value,
    key_cache,
    value_cache,
    lengths,
    residual,
    norm_gain,
    router,
    routes,
    w_gate,
    w_up,
    w_down,
):
    seqs, width = residual.shape
    experts = router.shape[1]
    side = lax.axis_size("side")
    members = side // experts
    cap = seqs // 2
    cuts = TILE // cap
    piece = width // cuts
    each = experts * cap
    pair = min(2, members)
    heads = width // HD
    vmem = pl.BlockSpec(memory_space=pltpu.VMEM)
    hbm = pl.BlockSpec(memory_space=pltpu.HBM)
    dma = pltpu.SemaphoreType.DMA
    return pl.pallas_call(
        functools.partial(kernel, side),
        out_shape=jax.ShapeDtypeStruct((seqs, width), BF16),
        in_specs=[hbm] * 13,
        out_specs=vmem,
        scratch_shapes=[
            pltpu.VMEM(query.shape, BF16),
            pltpu.VMEM(new_key.shape, BF16),
            pltpu.VMEM(new_value.shape, BF16),
            pltpu.SMEM(lengths.shape, jnp.int32),
            pltpu.VMEM(residual.shape, BF16),
            pltpu.VMEM(norm_gain.shape, BF16),
            pltpu.VMEM((experts, width), BF16),
            pltpu.VMEM((2, seqs), jnp.int32),
            pltpu.VMEM(key_cache.shape, BF16),
            pltpu.VMEM(value_cache.shape, BF16),
            pltpu.VMEM(w_gate.shape, BF16),
            pltpu.VMEM(w_up.shape, BF16),
            pltpu.VMEM(w_down.shape, BF16),
            pltpu.VMEM((seqs * heads, HD), F32),
            pltpu.VMEM((seqs * heads, HD), F32),
            pltpu.VMEM((experts, TILE, piece), BF16),
            pltpu.VMEM((members, experts, TILE, piece), BF16),
            pltpu.VMEM((members // pair, pair * each, w_gate.shape[1]), BF16),
            pltpu.VMEM((members, cuts, each, piece), F32),
            pltpu.VMEM((members, cuts, each, piece), BF16),
            pltpu.VMEM((members, cuts, each, piece), BF16),
            pltpu.VMEM((experts, TILE, piece), BF16),
            pltpu.VMEM((experts, TILE, piece), BF16),
            dma((13,)),
            dma((experts - 1,)),
            dma((experts,)),
            dma((members, experts)),
            dma((members, experts)),
            dma((members, cuts)),
            dma((members, cuts)),
            dma((experts - 1,)),
            dma((experts,)),
        ],
        compiler_params=pltpu.CompilerParams(
            collective_id=0, has_side_effects=True, vmem_limit_bytes=64 * 1024 * 1024
        ),
    )(
        query,
        new_key,
        new_value,
        lengths,
        residual,
        norm_gain,
        router.T,
        routes.T,
        key_cache,
        value_cache,
        w_gate,
        w_up,
        w_down,
    )


def solution(mesh):
    in_specs = (
        P(("groups", "side"), None),
        P(("groups", "side"), None),
        P(("groups", "side"), None),
        P(("groups", "side"), None, None),
        P(("groups", "side"), None, None),
        P(("groups", "side")),
        P(("groups", "side"), None),
        P(),
        P(),
        P(("groups", "side"), None),
        P(None, "side"),
        P(None, "side"),
        P("side", None),
    )
    out_specs = P(("groups", "side"), None)
    return jax.shard_map(
        on_device, mesh=mesh, in_specs=in_specs, out_specs=out_specs, check_vma=False
    )
```

```python
import functools

import jax
import jax.numpy as jnp
from jax import lax
from jax.experimental import pallas as pl
from jax.experimental.pallas import tpu as pltpu
from jax.sharding import PartitionSpec as P

HD = 128
TILE = 16
PART = 256
F32 = jnp.float32
BF16 = jnp.bfloat16
MESH = pl.DeviceIdType.MESH


def dot(a, b):
    return jnp.dot(a, b, preferred_element_type=F32)


def iota(shape, dim):
    return lax.broadcasted_iota(jnp.int32, shape, dim)


def attend(query_ref, new_key_ref, new_value_ref, lengths_ref, keys, values, values_ready, q_rows, o_rows):
    seqs, width = query_ref.shape
    kv = new_key_ref.shape[1]
    heads = width // HD
    group = width // kv
    slots = keys.shape[1]
    scale = HD ** (-0.5)
    query = query_ref[...].astype(F32)
    for h in range(heads):
        q_rows[pl.ds(h, seqs, stride=heads), :] = query[:, h * HD : (h + 1) * HD]
    own_keys = new_key_ref[...].astype(F32)
    mine = iota((heads, kv), 0) // group == iota((heads, kv), 1) // HD
    position = iota((heads, slots), 1)
    scores, own = [], []
    for s in range(seqs):
        q = q_rows[s * heads : (s + 1) * heads, :]
        wide = jnp.where(mine, jnp.concatenate([q] * (kv // HD), axis=1), 0.0)
        score = lax.dot_general(
            wide.astype(BF16), keys[s], (((1,), (1,)), ((), ())), preferred_element_type=F32
        )
        scores.append(jnp.where(position < lengths_ref[s], score * scale, -jnp.inf))
        own.append(jnp.sum(wide * own_keys[s : s + 1, :], axis=1, keepdims=True) * scale)
    values_ready()
    own_values = new_value_ref[...].astype(F32)
    for s in range(seqs):
        top = jnp.maximum(jnp.max(scores[s], axis=1, keepdims=True), own[s])
        weights = jnp.exp(scores[s] - top)
        own_weight = jnp.exp(own[s] - top)
        total = jnp.sum(weights, axis=1, keepdims=True) + own_weight
        mixed = dot(weights.astype(BF16), values[s])
        mixed = mixed + own_weight.astype(BF16).astype(F32) * own_values[s : s + 1, :]
        mixed = jnp.where(mine, mixed, 0.0)
        summed = mixed[:, :HD]
        for j in range(1, kv // HD):
            summed = summed + mixed[:, j * HD : (j + 1) * HD]
        o_rows[s * heads : (s + 1) * heads, :] = summed / total
    return jnp.concatenate(
        [o_rows[pl.ds(h, seqs, stride=heads), :] for h in range(heads)], axis=1
    )


def kernel(
    side,
    query_hbm,
    new_key_hbm,
    new_value_hbm,
    lengths_hbm,
    residual_hbm,
    gain_hbm,
    router_hbm,
    routes_hbm,
    key_hbm,
    value_hbm,
    gate_hbm,
    up_hbm,
    down_hbm,
    out_ref,
    query_ref,
    new_key_ref,
    new_value_ref,
    lengths_ref,
    residual_ref,
    gain_ref,
    router_ref,
    routes_ref,
    keys,
    values,
    w_gate,
    w_up,
    w_down,
    q_rows,
    o_rows,
    packed,
    arrived,
    hidden,
    partial,
    part_out,
    part_in,
    back_out,
    back_in,
    load_sem,
    send_sem,
    recv_sem,
    fsend_sem,
    frecv_sem,
    psend_sem,
    precv_sem,
    rsend_sem,
    rrecv_sem,
):
    seqs, width = residual_hbm.shape
    experts = router_hbm.shape[0]
    members = side // experts
    cap = seqs // 2
    cuts = TILE // cap
    piece = width // cuts
    rows = experts * TILE
    each = experts * cap
    me = lax.axis_index("side")
    chip = me // members
    lane = lax.rem(me, members)

    loads = []
    for n, (src, dst) in enumerate(
        (
            (routes_hbm, routes_ref),
            (query_hbm, query_ref),
            (lengths_hbm, lengths_ref),
            (new_key_hbm, new_key_ref),
            (key_hbm, keys),
            (new_value_hbm, new_value_ref),
            (value_hbm, values),
            (residual_hbm, residual_ref),
            (gain_hbm, gain_ref),
            (router_hbm, router_ref),
            (gate_hbm, w_gate),
            (up_hbm, w_up),
            (down_hbm, w_down),
        )
    ):
        load = pltpu.make_async_copy(src, dst, load_sem.at[n])
        if n < 10:
            load.start()
        loads.append(load)

    others = [lax.rem(chip + d, experts) for d in range(1, experts)]
    mates = [lax.rem(lane + j, members) for j in range(1, members)]
    barrier = pltpu.get_barrier_semaphore()
    for other in others:
        pl.semaphore_signal(
            barrier, inc=1, device_id={"side": other * members + lane}, device_id_type=MESH
        )
    for mate in mates:
        pl.semaphore_signal(
            barrier, inc=1, device_id={"side": chip * members + mate}, device_id_type=MESH
        )

    ids = iota((seqs, experts), 1)
    loads[0].wait()
    diagonal = iota((seqs, seqs), 0) == iota((seqs, seqs), 1)
    first_hot, second_hot = [
        (
            jnp.sum(jnp.where(diagonal, routes_ref[n : n + 1, :], 0), axis=1, keepdims=True) == ids
        ).astype(F32)
        for n in range(2)
    ]
    routed = (first_hot + second_hot).astype(BF16)
    earlier = (iota((seqs, seqs), 0) > iota((seqs, seqs), 1)).astype(BF16)
    rank = dot(earlier, routed).astype(BF16)
    spread = (iota((experts, rows), 0) == iota((experts, rows), 1) // TILE).astype(BF16)
    slot = lax.rem(iota((seqs, rows), 1), cap).astype(F32)
    chosen = jnp.where(dot(rank, spread) == slot, dot(routed, spread), 0.0)
    cut_mask = iota((cuts * seqs, rows), 0) // seqs == lax.rem(
        iota((cuts * seqs, rows), 1) // cap, cuts
    )
    select = jnp.where(cut_mask, jnp.concatenate([chosen] * cuts, axis=0), 0.0)

    for load in loads[1:5]:
        load.wait()
    for load in loads[10:]:
        load.start()

    def values_ready():
        for load in loads[5:10]:
            load.wait()

    attention = attend(
        query_ref, new_key_ref, new_value_ref, lengths_ref, keys, values, values_ready, q_rows, o_rows
    )
    mid = (residual_ref[...].astype(F32) + attention).astype(BF16).astype(F32)
    normed = (
        mid
        * lax.rsqrt(jnp.mean(mid * mid, axis=1, keepdims=True) + 1e-05)
        * gain_ref[...].astype(F32).reshape(1, width)
    )
    stacked = jnp.concatenate(
        [normed[:, b * piece : (b + 1) * piece] for b in range(cuts)], axis=0
    ).astype(BF16)
    packed[...] = (
        dot(select.T.astype(BF16), stacked).astype(BF16).reshape(experts, TILE, piece)
    )

    pl.semaphore_wait(barrier, len(others) + len(mates))
    sends = []
    for d, other in enumerate(others):
        copy = pltpu.make_async_remote_copy(
            src_ref=packed.at[other],
            dst_ref=arrived.at[lane, chip],
            send_sem=send_sem.at[d],
            recv_sem=recv_sem.at[chip],
            device_id={"side": other * members + lane},
            device_id_type=MESH,
        )
        copy.start()
        sends.append(copy)
    arrived[lane, chip] = packed[chip]

    def forward(d, source):
        for j, mate in enumerate(mates):
            copy = pltpu.make_async_remote_copy(
                src_ref=arrived.at[lane, source],
                dst_ref=arrived.at[lane, source],
                send_sem=fsend_sem.at[j, d],
                recv_sem=frecv_sem.at[lane, source],
                device_id={"side": chip * members + mate},
                device_id_type=MESH,
            )
            copy.start()
            sends.append(copy)

    forward(0, chip)

    logits = lax.dot_general(
        normed.astype(BF16), router_ref[...], (((1,), (1,)), ((), ())), preferred_element_type=F32
    )
    gap = jnp.sum((first_hot - second_hot) * logits, axis=1, keepdims=True)
    gates = first_hot * jax.nn.sigmoid(gap) + second_hot * jax.nn.sigmoid(-gap)
    combine = (
        jnp.where(cut_mask, jnp.concatenate([dot(gates.astype(BF16), spread)] * cuts, axis=0), 0.0)
        * select
    ).astype(BF16)

    r, q = iota((rows, rows), 0), iota((rows, rows), 1)
    order = (
        lax.rem(r, each) // cap * TILE + r // each * cap + lax.rem(r, cap) == q
    ).astype(BF16)

    def sources():
        return [(d, lax.rem(chip + experts - d, experts)) for d in range(1, experts)]

    for d, source in sources():
        pltpu.make_async_remote_copy(
            src_ref=packed.at[source],
            dst_ref=arrived.at[lane, source],
            send_sem=send_sem.at[d - 1],
            recv_sem=recv_sem.at[source],
            device_id={"side": source * members + lane},
            device_id_type=MESH,
        ).wait_recv()
        forward(d, source)
    for load in loads[10:]:
        load.wait()
    for d, source in [(0, chip)] + sources():
        for j, mate in enumerate(mates):
            pltpu.make_async_remote_copy(
                src_ref=arrived.at[mate, source],
                dst_ref=arrived.at[mate, source],
                send_sem=fsend_sem.at[j, d],
                recv_sem=frecv_sem.at[mate, source],
                device_id={"side": chip * members + mate},
                device_id_type=MESH,
            ).wait_recv()

    parts = partial.shape[1]
    wide = piece // parts

    def give(p):
        for j, mate in enumerate(mates):
            copy = pltpu.make_async_remote_copy(
                src_ref=part_out.at[mate, p],
                dst_ref=part_in.at[lane, p],
                send_sem=psend_sem.at[j, p],
                recv_sem=precv_sem.at[lane, p],
                device_id={"side": chip * members + mate},
                device_id_type=MESH,
            )
            copy.start()
            sends.append(copy)

    pair = min(2, members)
    blocks = members // pair

    def expand(block):
        tokens = [
            dot(order, arrived[block * pair + n].reshape(rows, piece)).astype(BF16)
            for n in range(pair)
        ]
        gate_part = up_part = 0.0
        for b in range(cuts):
            x = jnp.concatenate([t[b * each : (b + 1) * each] for t in tokens], axis=0)
            gate_part = gate_part + dot(x, w_gate[b * piece : (b + 1) * piece, :])
            up_part = up_part + dot(x, w_up[b * piece : (b + 1) * piece, :])
        hidden[block] = (jax.nn.silu(gate_part) * up_part).astype(BF16)

    def contract(block, p):
        for b in range(cuts):
            start = b * piece + p * wide
            y = dot(hidden[block], w_down[:, start : start + wide]).reshape(pair, each, wide)
            for n in range(pair):
                partial[block * pair + n, p, b * each : (b + 1) * each, :] = y[n]
                part_out[block * pair + n, p, b * each : (b + 1) * each, :] = y[n].astype(BF16)

    def over(fn):
        if blocks == 1:
            fn(0)
        else:
            pl.loop(0, blocks)(fn)

    order_back = (
        lax.rem(q, each) // cap * TILE + q // each * cap + lax.rem(q, cap) == r
    ).astype(BF16)

    def collect(p):
        total = partial[lane, p]
        for j, mate in enumerate(mates):
            pltpu.make_async_remote_copy(
                src_ref=part_out.at[mate, p],
                dst_ref=part_in.at[mate, p],
                send_sem=psend_sem.at[j, p],
                recv_sem=precv_sem.at[mate, p],
                device_id={"side": chip * members + mate},
                device_id_type=MESH,
            ).wait_recv()
            total = total + part_in[mate, p].astype(F32)
        back_out[p] = dot(order_back, total.astype(BF16)).astype(BF16).reshape(experts, TILE, wide)
        for d, other in enumerate(others):
            copy = pltpu.make_async_remote_copy(
                src_ref=back_out.at[p, other],
                dst_ref=back_in.at[p, chip],
                send_sem=rsend_sem.at[p, d],
                recv_sem=rrecv_sem.at[p, chip],
                device_id={"side": other * members + lane},
                device_id_type=MESH,
            )
            copy.start()
            sends.append(copy)
        back_in[p, chip] = back_out[p, chip]

    over(expand)
    for p in range(parts):
        over(functools.partial(contract, p=p))
        give(p)
        if p > 0:
            collect(p - 1)
    collect(parts - 1)

    for p in range(parts):
        for d, source in sources():
            pltpu.make_async_remote_copy(
                src_ref=back_out.at[p, source],
                dst_ref=back_in.at[p, source],
                send_sem=rsend_sem.at[p, d - 1],
                recv_sem=rrecv_sem.at[p, source],
                device_id={"side": source * members + lane},
                device_id_type=MESH,
            ).wait_recv()
        moe = dot(combine, back_in[p].reshape(rows, wide))
        for b in range(cuts):
            columns = slice(b * piece + p * wide, b * piece + (p + 1) * wide)
            out_ref[:, columns] = (mid[:, columns] + moe[b * seqs : (b + 1) * seqs]).astype(BF16)
    for copy in sends:
        copy.wait_send()


def on_device(
    query,
    new_key,
    new_value,
    key_cache,
    value_cache,
    lengths,
    residual,
    norm_gain,
    router,
    routes,
    w_gate,
    w_up,
    w_down,
):
    seqs, width = residual.shape
    experts = router.shape[1]
    side = lax.axis_size("side")
    members = side // experts
    cap = seqs // 2
    cuts = TILE // cap
    piece = width // cuts
    each = experts * cap
    rows = experts * TILE
    parts = piece // PART
    wide = piece // parts
    pair = min(2, members)
    heads = width // HD
    vmem = pl.BlockSpec(memory_space=pltpu.VMEM)
    hbm = pl.BlockSpec(memory_space=pltpu.HBM)
    dma = pltpu.SemaphoreType.DMA
    return pl.pallas_call(
        functools.partial(kernel, side),
        out_shape=jax.ShapeDtypeStruct((seqs, width), BF16),
        in_specs=[hbm] * 13,
        out_specs=vmem,
        scratch_shapes=[
            pltpu.VMEM(query.shape, BF16),
            pltpu.VMEM(new_key.shape, BF16),
            pltpu.VMEM(new_value.shape, BF16),
            pltpu.SMEM(lengths.shape, jnp.int32),
            pltpu.VMEM(residual.shape, BF16),
            pltpu.VMEM(norm_gain.shape, BF16),
            pltpu.VMEM((experts, width), BF16),
            pltpu.VMEM((2, seqs), jnp.int32),
            pltpu.VMEM(key_cache.shape, BF16),
            pltpu.VMEM(value_cache.shape, BF16),
            pltpu.VMEM(w_gate.shape, BF16),
            pltpu.VMEM(w_up.shape, BF16),
            pltpu.VMEM(w_down.shape, BF16),
            pltpu.VMEM((seqs * heads, HD), F32),
            pltpu.VMEM((seqs * heads, HD), F32),
            pltpu.VMEM((experts, TILE, piece), BF16),
            pltpu.VMEM((members, experts, TILE, piece), BF16),
            pltpu.VMEM((members // pair, pair * each, w_gate.shape[1]), BF16),
            pltpu.VMEM((members, parts, rows, wide), F32),
            pltpu.VMEM((members, parts, rows, wide), BF16),
            pltpu.VMEM((members, parts, rows, wide), BF16),
            pltpu.VMEM((parts, experts, TILE, wide), BF16),
            pltpu.VMEM((parts, experts, TILE, wide), BF16),
            dma((13,)),
            dma((experts - 1,)),
            dma((experts,)),
            dma((members, experts)),
            dma((members, experts)),
            dma((members, parts)),
            dma((members, parts)),
            dma((parts, experts - 1)),
            dma((parts, experts)),
        ],
        compiler_params=pltpu.CompilerParams(
            collective_id=0, has_side_effects=True, vmem_limit_bytes=64 * 1024 * 1024
        ),
    )(
        query,
        new_key,
        new_value,
        lengths,
        residual,
        norm_gain,
        router.T,
        routes.T,
        key_cache,
        value_cache,
        w_gate,
        w_up,
        w_down,
    )


def solution(mesh):
    in_specs = (
        P(("groups", "side"), None),
        P(("groups", "side"), None),
        P(("groups", "side"), None),
        P(("groups", "side"), None, None),
        P(("groups", "side"), None, None),
        P(("groups", "side")),
        P(("groups", "side"), None),
        P(),
        P(),
        P(("groups", "side"), None),
        P(None, "side"),
        P(None, "side"),
        P("side", None),
    )
    out_specs = P(("groups", "side"), None)
    return jax.shard_map(
        on_device, mesh=mesh, in_specs=in_specs, out_specs=out_specs, check_vma=False
    )
```

```python
import functools

import jax
import jax.numpy as jnp
from jax import lax
from jax.experimental import pallas as pl
from jax.experimental.pallas import tpu as pltpu
from jax.sharding import PartitionSpec as P

HD = 128
TILE = 16
PART = 256
F32 = jnp.float32
BF16 = jnp.bfloat16
MESH = pl.DeviceIdType.MESH


def dot(a, b):
    return jnp.dot(a, b, preferred_element_type=F32)


def iota(shape, dim):
    return lax.broadcasted_iota(jnp.int32, shape, dim)


def attend(query_ref, new_key_ref, new_value_ref, lengths_ref, keys, values, values_ready, q_rows, o_rows):
    seqs, width = query_ref.shape
    kv = new_key_ref.shape[1]
    heads = width // HD
    group = width // kv
    slots = keys.shape[1]
    scale = HD ** (-0.5)
    query = query_ref[...].astype(F32)
    for h in range(heads):
        q_rows[pl.ds(h, seqs, stride=heads), :] = query[:, h * HD : (h + 1) * HD]
    own_keys = new_key_ref[...].astype(F32)
    mine = iota((heads, kv), 0) // group == iota((heads, kv), 1) // HD
    position = iota((heads, slots), 1)
    scores, own = [], []
    for s in range(seqs):
        q = q_rows[s * heads : (s + 1) * heads, :]
        wide = jnp.where(mine, jnp.concatenate([q] * (kv // HD), axis=1), 0.0)
        score = lax.dot_general(
            wide.astype(BF16), keys[s], (((1,), (1,)), ((), ())), preferred_element_type=F32
        )
        scores.append(jnp.where(position < lengths_ref[s], score * scale, -jnp.inf))
        own.append(jnp.sum(wide * own_keys[s : s + 1, :], axis=1, keepdims=True) * scale)
    values_ready()
    own_values = new_value_ref[...].astype(F32)
    for s in range(seqs):
        top = jnp.maximum(jnp.max(scores[s], axis=1, keepdims=True), own[s])
        weights = jnp.exp(scores[s] - top)
        own_weight = jnp.exp(own[s] - top)
        total = jnp.sum(weights, axis=1, keepdims=True) + own_weight
        mixed = dot(weights.astype(BF16), values[s])
        mixed = mixed + own_weight.astype(BF16).astype(F32) * own_values[s : s + 1, :]
        mixed = jnp.where(mine, mixed, 0.0)
        summed = mixed[:, :HD]
        for j in range(1, kv // HD):
            summed = summed + mixed[:, j * HD : (j + 1) * HD]
        o_rows[s * heads : (s + 1) * heads, :] = summed / total
    return jnp.concatenate(
        [o_rows[pl.ds(h, seqs, stride=heads), :] for h in range(heads)], axis=1
    )


def kernel(
    side,
    query_hbm,
    new_key_hbm,
    new_value_hbm,
    lengths_hbm,
    residual_hbm,
    gain_hbm,
    router_hbm,
    routes_hbm,
    key_hbm,
    value_hbm,
    gate_hbm,
    up_hbm,
    down_hbm,
    out_ref,
    query_ref,
    new_key_ref,
    new_value_ref,
    lengths_ref,
    residual_ref,
    gain_ref,
    router_ref,
    routes_ref,
    keys,
    values,
    w_gate,
    w_up,
    w_down,
    q_rows,
    o_rows,
    packed,
    arrived,
    hidden,
    partial,
    part_out,
    part_in,
    back_out,
    back_in,
    load_sem,
    send_sem,
    recv_sem,
    fsend_sem,
    frecv_sem,
    psend_sem,
    precv_sem,
    rsend_sem,
    rrecv_sem,
):
    seqs, width = residual_hbm.shape
    experts = router_hbm.shape[0]
    members = side // experts
    cap = seqs // 2
    cuts = TILE // cap
    piece = width // cuts
    rows = experts * TILE
    each = experts * cap
    me = lax.axis_index("side")
    chip = me // members
    lane = lax.rem(me, members)

    loads = []
    for n, (src, dst) in enumerate(
        (
            (routes_hbm, routes_ref),
            (query_hbm, query_ref),
            (lengths_hbm, lengths_ref),
            (new_key_hbm, new_key_ref),
            (key_hbm, keys),
            (new_value_hbm, new_value_ref),
            (value_hbm, values),
            (residual_hbm, residual_ref),
            (gain_hbm, gain_ref),
            (router_hbm, router_ref),
            (gate_hbm, w_gate),
            (up_hbm, w_up),
            (down_hbm, w_down),
        )
    ):
        load = pltpu.make_async_copy(src, dst, load_sem.at[n])
        if n < 10:
            load.start()
        loads.append(load)

    others = [lax.rem(chip + d, experts) for d in range(1, experts)]
    mates = [lax.rem(lane + j, members) for j in range(1, members)]
    barrier = pltpu.get_barrier_semaphore()
    for other in others:
        pl.semaphore_signal(
            barrier, inc=1, device_id={"side": other * members + lane}, device_id_type=MESH
        )
    for mate in mates:
        pl.semaphore_signal(
            barrier, inc=1, device_id={"side": chip * members + mate}, device_id_type=MESH
        )

    ids = iota((seqs, experts), 1)
    loads[0].wait()
    diagonal = iota((seqs, seqs), 0) == iota((seqs, seqs), 1)
    first_hot, second_hot = [
        (
            jnp.sum(jnp.where(diagonal, routes_ref[n : n + 1, :], 0), axis=1, keepdims=True) == ids
        ).astype(F32)
        for n in range(2)
    ]
    routed = (first_hot + second_hot).astype(BF16)
    earlier = (iota((seqs, seqs), 0) > iota((seqs, seqs), 1)).astype(BF16)
    rank = dot(earlier, routed).astype(BF16)
    spread = (iota((experts, rows), 0) == iota((experts, rows), 1) // TILE).astype(BF16)
    slot = lax.rem(iota((seqs, rows), 1), cap).astype(F32)
    chosen = jnp.where(dot(rank, spread) == slot, dot(routed, spread), 0.0)
    cut_mask = iota((cuts * seqs, rows), 0) // seqs == lax.rem(
        iota((cuts * seqs, rows), 1) // cap, cuts
    )
    select = jnp.where(cut_mask, jnp.concatenate([chosen] * cuts, axis=0), 0.0)

    for load in loads[1:5]:
        load.wait()
    for load in loads[10:]:
        load.start()

    def values_ready():
        for load in loads[5:10]:
            load.wait()

    attention = attend(
        query_ref, new_key_ref, new_value_ref, lengths_ref, keys, values, values_ready, q_rows, o_rows
    )
    mid = (residual_ref[...].astype(F32) + attention).astype(BF16).astype(F32)
    normed = (
        mid
        * lax.rsqrt(jnp.mean(mid * mid, axis=1, keepdims=True) + 1e-05)
        * gain_ref[...].astype(F32).reshape(1, width)
    )
    stacked = jnp.concatenate(
        [normed[:, b * piece : (b + 1) * piece] for b in range(cuts)], axis=0
    ).astype(BF16)
    packed[...] = (
        dot(select.T.astype(BF16), stacked).astype(BF16).reshape(experts, TILE, piece)
    )

    pl.semaphore_wait(barrier, len(others) + len(mates))
    sends = []
    for d, other in enumerate(others):
        copy = pltpu.make_async_remote_copy(
            src_ref=packed.at[other],
            dst_ref=arrived.at[lane, chip],
            send_sem=send_sem.at[d],
            recv_sem=recv_sem.at[chip],
            device_id={"side": other * members + lane},
            device_id_type=MESH,
        )
        copy.start()
        sends.append(copy)
    arrived[lane, chip] = packed[chip]

    def forward(d, source):
        for j, mate in enumerate(mates):
            copy = pltpu.make_async_remote_copy(
                src_ref=arrived.at[lane, source],
                dst_ref=arrived.at[lane, source],
                send_sem=fsend_sem.at[j, d],
                recv_sem=frecv_sem.at[lane, source],
                device_id={"side": chip * members + mate},
                device_id_type=MESH,
            )
            copy.start()
            sends.append(copy)

    forward(0, chip)

    logits = lax.dot_general(
        normed.astype(BF16), router_ref[...], (((1,), (1,)), ((), ())), preferred_element_type=F32
    )
    gap = jnp.sum((first_hot - second_hot) * logits, axis=1, keepdims=True)
    gates = first_hot * jax.nn.sigmoid(gap) + second_hot * jax.nn.sigmoid(-gap)
    combine = (
        jnp.where(cut_mask, jnp.concatenate([dot(gates.astype(BF16), spread)] * cuts, axis=0), 0.0)
        * select
    ).astype(BF16)

    r, q = iota((rows, rows), 0), iota((rows, rows), 1)
    order = (
        lax.rem(r, each) // cap * TILE + r // each * cap + lax.rem(r, cap) == q
    ).astype(BF16)

    def sources():
        return [(d, lax.rem(chip + experts - d, experts)) for d in range(1, experts)]

    for d, source in sources():
        pltpu.make_async_remote_copy(
            src_ref=packed.at[source],
            dst_ref=arrived.at[lane, source],
            send_sem=send_sem.at[d - 1],
            recv_sem=recv_sem.at[source],
            device_id={"side": source * members + lane},
            device_id_type=MESH,
        ).wait_recv()
        forward(d, source)
    for load in loads[10:]:
        load.wait()
    for d, source in [(0, chip)] + sources():
        for j, mate in enumerate(mates):
            pltpu.make_async_remote_copy(
                src_ref=arrived.at[mate, source],
                dst_ref=arrived.at[mate, source],
                send_sem=fsend_sem.at[j, d],
                recv_sem=frecv_sem.at[mate, source],
                device_id={"side": chip * members + mate},
                device_id_type=MESH,
            ).wait_recv()

    parts = partial.shape[1]
    wide = piece // parts

    def give(p):
        for j, mate in enumerate(mates):
            copy = pltpu.make_async_remote_copy(
                src_ref=part_out.at[mate, p],
                dst_ref=part_in.at[lane, p],
                send_sem=psend_sem.at[j, p],
                recv_sem=precv_sem.at[lane, p],
                device_id={"side": chip * members + mate},
                device_id_type=MESH,
            )
            copy.start()
            sends.append(copy)

    pair = min(2, members)
    blocks = members // pair

    def expand(block):
        tokens = [
            dot(order, arrived[block * pair + n].reshape(rows, piece)).astype(BF16)
            for n in range(pair)
        ]
        gate_part = up_part = 0.0
        for b in range(cuts):
            x = jnp.concatenate([t[b * each : (b + 1) * each] for t in tokens], axis=0)
            gate_part = gate_part + dot(x, w_gate[b * piece : (b + 1) * piece, :])
            up_part = up_part + dot(x, w_up[b * piece : (b + 1) * piece, :])
        hidden[block] = (jax.nn.silu(gate_part) * up_part).astype(BF16)

    def contract(block, p):
        for b in range(cuts):
            start = b * piece + p * wide
            y = dot(hidden[block], w_down[:, start : start + wide]).reshape(pair, each, wide)
            for n in range(pair):
                partial[block * pair + n, p, b * each : (b + 1) * each, :] = y[n]
                part_out[block * pair + n, p, b * each : (b + 1) * each, :] = y[n].astype(BF16)

    def over(fn):
        if blocks == 1:
            fn(0)
        else:
            pl.loop(0, blocks)(fn)

    order_back = (
        lax.rem(q, each) // cap * TILE + q // each * cap + lax.rem(q, cap) == r
    ).astype(BF16)

    def collect(p):
        total = partial[lane, p]
        for j, mate in enumerate(mates):
            pltpu.make_async_remote_copy(
                src_ref=part_out.at[mate, p],
                dst_ref=part_in.at[mate, p],
                send_sem=psend_sem.at[j, p],
                recv_sem=precv_sem.at[mate, p],
                device_id={"side": chip * members + mate},
                device_id_type=MESH,
            ).wait_recv()
            total = total + part_in[mate, p].astype(F32)
        back_out[p] = dot(order_back, total.astype(BF16)).astype(BF16).reshape(experts, TILE, wide)
        for d, other in enumerate(others):
            copy = pltpu.make_async_remote_copy(
                src_ref=back_out.at[p, other],
                dst_ref=back_in.at[p, chip],
                send_sem=rsend_sem.at[p, d],
                recv_sem=rrecv_sem.at[p, chip],
                device_id={"side": other * members + lane},
                device_id_type=MESH,
            )
            copy.start()
            sends.append(copy)
        back_in[p, chip] = back_out[p, chip]

    over(expand)
    for p in range(parts):
        over(functools.partial(contract, p=p))
        give(p)
        if p > 0:
            collect(p - 1)
    collect(parts - 1)

    for p in range(parts):
        for d, source in sources():
            pltpu.make_async_remote_copy(
                src_ref=back_out.at[p, source],
                dst_ref=back_in.at[p, source],
                send_sem=rsend_sem.at[p, d - 1],
                recv_sem=rrecv_sem.at[p, source],
                device_id={"side": source * members + lane},
                device_id_type=MESH,
            ).wait_recv()
        moe = dot(combine, back_in[p].reshape(rows, wide))
        for b in range(cuts):
            columns = slice(b * piece + p * wide, b * piece + (p + 1) * wide)
            out_ref[:, columns] = (mid[:, columns] + moe[b * seqs : (b + 1) * seqs]).astype(BF16)
    for copy in sends:
        copy.wait_send()


def on_device(
    query,
    new_key,
    new_value,
    key_cache,
    value_cache,
    lengths,
    residual,
    norm_gain,
    router,
    routes,
    w_gate,
    w_up,
    w_down,
):
    seqs, width = residual.shape
    experts = router.shape[1]
    side = lax.axis_size("side")
    members = side // experts
    cap = seqs // 2
    cuts = TILE // cap
    piece = width // cuts
    each = experts * cap
    rows = experts * TILE
    parts = piece // PART
    wide = piece // parts
    pair = min(2, members)
    heads = width // HD
    vmem = pl.BlockSpec(memory_space=pltpu.VMEM)
    hbm = pl.BlockSpec(memory_space=pltpu.HBM)
    dma = pltpu.SemaphoreType.DMA
    return pl.pallas_call(
        functools.partial(kernel, side),
        out_shape=pltpu.VMEM((seqs, width), BF16),
        in_specs=[hbm] * 13,
        out_specs=vmem,
        scratch_shapes=[
            pltpu.VMEM(query.shape, BF16),
            pltpu.VMEM(new_key.shape, BF16),
            pltpu.VMEM(new_value.shape, BF16),
            pltpu.SMEM(lengths.shape, jnp.int32),
            pltpu.VMEM(residual.shape, BF16),
            pltpu.VMEM(norm_gain.shape, BF16),
            pltpu.VMEM((experts, width), BF16),
            pltpu.VMEM((2, seqs), jnp.int32),
            pltpu.VMEM(key_cache.shape, BF16),
            pltpu.VMEM(value_cache.shape, BF16),
            pltpu.VMEM(w_gate.shape, BF16),
            pltpu.VMEM(w_up.shape, BF16),
            pltpu.VMEM(w_down.shape, BF16),
            pltpu.VMEM((seqs * heads, HD), F32),
            pltpu.VMEM((seqs * heads, HD), F32),
            pltpu.VMEM((experts, TILE, piece), BF16),
            pltpu.VMEM((members, experts, TILE, piece), BF16),
            pltpu.VMEM((members // pair, pair * each, w_gate.shape[1]), BF16),
            pltpu.VMEM((members, parts, rows, wide), F32),
            pltpu.VMEM((members, parts, rows, wide), BF16),
            pltpu.VMEM((members, parts, rows, wide), BF16),
            pltpu.VMEM((parts, experts, TILE, wide), BF16),
            pltpu.VMEM((parts, experts, TILE, wide), BF16),
            dma((13,)),
            dma((experts - 1,)),
            dma((experts,)),
            dma((members, experts)),
            dma((members, experts)),
            dma((members, parts)),
            dma((members, parts)),
            dma((parts, experts - 1)),
            dma((parts, experts)),
        ],
        compiler_params=pltpu.CompilerParams(
            collective_id=0, has_side_effects=True, vmem_limit_bytes=56 * 1024 * 1024
        ),
    )(
        *[
            pltpu.with_memory_space_constraint(x, pltpu.HBM)
            for x in (
                query,
                new_key,
                new_value,
                lengths,
                residual,
                norm_gain,
                router.T,
                routes.T,
                key_cache,
                value_cache,
                w_gate,
                w_up,
                w_down,
            )
        ]
    )


def solution(mesh):
    in_specs = (
        P(("groups", "side"), None),
        P(("groups", "side"), None),
        P(("groups", "side"), None),
        P(("groups", "side"), None, None),
        P(("groups", "side"), None, None),
        P(("groups", "side")),
        P(("groups", "side"), None),
        P(),
        P(),
        P(("groups", "side"), None),
        P(None, "side"),
        P(None, "side"),
        P("side", None),
    )
    out_specs = P(("groups", "side"), None)
    return jax.shard_map(
        on_device, mesh=mesh, in_specs=in_specs, out_specs=out_specs, check_vma=False
    )
```

```python
import functools

import jax
import jax.numpy as jnp
from jax import lax
from jax.experimental import pallas as pl
from jax.experimental.pallas import tpu as pltpu
from jax.sharding import PartitionSpec as P

HD = 128
TILE = 16
PART = 384
F32 = jnp.float32
BF16 = jnp.bfloat16
MESH = pl.DeviceIdType.MESH


def dot(a, b):
    return jnp.dot(a, b, preferred_element_type=F32)


def iota(shape, dim):
    return lax.broadcasted_iota(jnp.int32, shape, dim)


def attend(query_ref, new_key_ref, new_value_ref, lengths_ref, keys, values, values_ready, q_rows, o_rows):
    seqs, width = query_ref.shape
    kv = new_key_ref.shape[1]
    heads = width // HD
    group = width // kv
    slots = keys.shape[1]
    scale = HD ** (-0.5)
    query = query_ref[...].astype(F32)
    for h in range(heads):
        q_rows[pl.ds(h, seqs, stride=heads), :] = query[:, h * HD : (h + 1) * HD]
    own_keys = new_key_ref[...].astype(F32)
    mine = iota((heads, kv), 0) // group == iota((heads, kv), 1) // HD
    position = iota((heads, slots), 1)
    scores, own = [], []
    for s in range(seqs):
        q = q_rows[s * heads : (s + 1) * heads, :]
        wide = jnp.where(mine, jnp.concatenate([q] * (kv // HD), axis=1), 0.0)
        score = lax.dot_general(
            wide.astype(BF16), keys[s], (((1,), (1,)), ((), ())), preferred_element_type=F32
        )
        scores.append(jnp.where(position < lengths_ref[s], score * scale, -jnp.inf))
        own.append(jnp.sum(wide * own_keys[s : s + 1, :], axis=1, keepdims=True) * scale)
    values_ready()
    own_values = new_value_ref[...].astype(F32)
    for s in range(seqs):
        top = jnp.maximum(jnp.max(scores[s], axis=1, keepdims=True), own[s])
        weights = jnp.exp(scores[s] - top)
        own_weight = jnp.exp(own[s] - top)
        total = jnp.sum(weights, axis=1, keepdims=True) + own_weight
        mixed = dot(weights.astype(BF16), values[s])
        mixed = mixed + own_weight.astype(BF16).astype(F32) * own_values[s : s + 1, :]
        mixed = jnp.where(mine, mixed, 0.0)
        summed = mixed[:, :HD]
        for j in range(1, kv // HD):
            summed = summed + mixed[:, j * HD : (j + 1) * HD]
        o_rows[s * heads : (s + 1) * heads, :] = summed / total
    return jnp.concatenate(
        [o_rows[pl.ds(h, seqs, stride=heads), :] for h in range(heads)], axis=1
    )


def kernel(
    side,
    query_hbm,
    new_key_hbm,
    new_value_hbm,
    lengths_hbm,
    residual_hbm,
    gain_hbm,
    router_hbm,
    routes_hbm,
    key_hbm,
    value_hbm,
    gate_hbm,
    up_hbm,
    down_hbm,
    out_ref,
    query_ref,
    new_key_ref,
    new_value_ref,
    lengths_ref,
    residual_ref,
    gain_ref,
    router_ref,
    routes_ref,
    keys,
    values,
    w_gate,
    w_up,
    w_down,
    q_rows,
    o_rows,
    packed,
    arrived,
    hidden,
    partial,
    part_out,
    part_in,
    back_out,
    back_in,
    load_sem,
    send_sem,
    recv_sem,
    fsend_sem,
    frecv_sem,
    psend_sem,
    precv_sem,
    rsend_sem,
    rrecv_sem,
):
    seqs, width = residual_hbm.shape
    experts = router_hbm.shape[0]
    members = side // experts
    cap = seqs // 2
    cuts = TILE // cap
    piece = width // cuts
    rows = experts * TILE
    each = experts * cap
    me = lax.axis_index("side")
    chip = me // members
    lane = lax.rem(me, members)

    loads = []
    for n, (src, dst) in enumerate(
        (
            (routes_hbm, routes_ref),
            (query_hbm, query_ref),
            (lengths_hbm, lengths_ref),
            (new_key_hbm, new_key_ref),
            (key_hbm, keys),
            (new_value_hbm, new_value_ref),
            (value_hbm, values),
            (residual_hbm, residual_ref),
            (gain_hbm, gain_ref),
            (router_hbm, router_ref),
            (gate_hbm, w_gate),
            (up_hbm, w_up),
            (down_hbm, w_down),
        )
    ):
        load = pltpu.make_async_copy(src, dst, load_sem.at[n])
        if n < 10:
            load.start()
        loads.append(load)

    others = [lax.rem(chip + d, experts) for d in range(1, experts)]
    mates = [lax.rem(lane + j, members) for j in range(1, members)]
    barrier = pltpu.get_barrier_semaphore()
    for other in others:
        pl.semaphore_signal(
            barrier, inc=1, device_id={"side": other * members + lane}, device_id_type=MESH
        )
    for mate in mates:
        pl.semaphore_signal(
            barrier, inc=1, device_id={"side": chip * members + mate}, device_id_type=MESH
        )

    ids = iota((seqs, experts), 1)
    loads[0].wait()
    diagonal = iota((seqs, seqs), 0) == iota((seqs, seqs), 1)
    first_hot, second_hot = [
        (
            jnp.sum(jnp.where(diagonal, routes_ref[n : n + 1, :], 0), axis=1, keepdims=True) == ids
        ).astype(F32)
        for n in range(2)
    ]
    routed = (first_hot + second_hot).astype(BF16)
    earlier = (iota((seqs, seqs), 0) > iota((seqs, seqs), 1)).astype(BF16)
    rank = dot(earlier, routed).astype(BF16)
    spread = (iota((experts, rows), 0) == iota((experts, rows), 1) // TILE).astype(BF16)
    slot = lax.rem(iota((seqs, rows), 1), cap).astype(F32)
    chosen = jnp.where(dot(rank, spread) == slot, dot(routed, spread), 0.0)
    cut_mask = iota((cuts * seqs, rows), 0) // seqs == lax.rem(
        iota((cuts * seqs, rows), 1) // cap, cuts
    )
    select = jnp.where(cut_mask, jnp.concatenate([chosen] * cuts, axis=0), 0.0)

    for load in loads[1:5]:
        load.wait()
    for load in loads[10:]:
        load.start()

    def values_ready():
        for load in loads[5:10]:
            load.wait()

    attention = attend(
        query_ref, new_key_ref, new_value_ref, lengths_ref, keys, values, values_ready, q_rows, o_rows
    )
    mid = (residual_ref[...].astype(F32) + attention).astype(BF16).astype(F32)
    normed = (
        mid
        * lax.rsqrt(jnp.mean(mid * mid, axis=1, keepdims=True) + 1e-05)
        * gain_ref[...].astype(F32).reshape(1, width)
    )
    stacked = jnp.concatenate(
        [normed[:, b * piece : (b + 1) * piece] for b in range(cuts)], axis=0
    ).astype(BF16)
    packed[...] = (
        dot(select.T.astype(BF16), stacked).astype(BF16).reshape(experts, TILE, piece)
    )

    pl.semaphore_wait(barrier, len(others) + len(mates))
    sends = []
    for d, other in enumerate(others):
        copy = pltpu.make_async_remote_copy(
            src_ref=packed.at[other],
            dst_ref=arrived.at[lane, chip],
            send_sem=send_sem.at[d],
            recv_sem=recv_sem.at[chip],
            device_id={"side": other * members + lane},
            device_id_type=MESH,
        )
        copy.start()
        sends.append(copy)
    arrived[lane, chip] = packed[chip]

    def forward(d, source):
        for j, mate in enumerate(mates):
            copy = pltpu.make_async_remote_copy(
                src_ref=arrived.at[lane, source],
                dst_ref=arrived.at[lane, source],
                send_sem=fsend_sem.at[j, d],
                recv_sem=frecv_sem.at[lane, source],
                device_id={"side": chip * members + mate},
                device_id_type=MESH,
            )
            copy.start()
            sends.append(copy)

    forward(0, chip)

    logits = lax.dot_general(
        normed.astype(BF16), router_ref[...], (((1,), (1,)), ((), ())), preferred_element_type=F32
    )
    gap = jnp.sum((first_hot - second_hot) * logits, axis=1, keepdims=True)
    gates = first_hot * jax.nn.sigmoid(gap) + second_hot * jax.nn.sigmoid(-gap)
    combine = (
        jnp.where(cut_mask, jnp.concatenate([dot(gates.astype(BF16), spread)] * cuts, axis=0), 0.0)
        * select
    ).astype(BF16)

    r, q = iota((rows, rows), 0), iota((rows, rows), 1)
    order = (
        lax.rem(r, each) // cap * TILE + r // each * cap + lax.rem(r, cap) == q
    ).astype(BF16)

    def sources():
        return [(d, lax.rem(chip + experts - d, experts)) for d in range(1, experts)]

    for d, source in sources():
        pltpu.make_async_remote_copy(
            src_ref=packed.at[source],
            dst_ref=arrived.at[lane, source],
            send_sem=send_sem.at[d - 1],
            recv_sem=recv_sem.at[source],
            device_id={"side": source * members + lane},
            device_id_type=MESH,
        ).wait_recv()
        forward(d, source)
    for load in loads[10:]:
        load.wait()
    for d, source in [(0, chip)] + sources():
        for j, mate in enumerate(mates):
            pltpu.make_async_remote_copy(
                src_ref=arrived.at[mate, source],
                dst_ref=arrived.at[mate, source],
                send_sem=fsend_sem.at[j, d],
                recv_sem=frecv_sem.at[mate, source],
                device_id={"side": chip * members + mate},
                device_id_type=MESH,
            ).wait_recv()

    parts = partial.shape[1]
    wide = piece // parts

    def give(p):
        for j, mate in enumerate(mates):
            copy = pltpu.make_async_remote_copy(
                src_ref=part_out.at[mate, p],
                dst_ref=part_in.at[lane, p],
                send_sem=psend_sem.at[j, p],
                recv_sem=precv_sem.at[lane, p],
                device_id={"side": chip * members + mate},
                device_id_type=MESH,
            )
            copy.start()
            sends.append(copy)

    pair = min(2, members)
    blocks = members // pair

    def expand(block):
        tokens = [
            dot(order, arrived[block * pair + n].reshape(rows, piece)).astype(BF16)
            for n in range(pair)
        ]
        gate_part = up_part = 0.0
        for b in range(cuts):
            x = jnp.concatenate([t[b * each : (b + 1) * each] for t in tokens], axis=0)
            gate_part = gate_part + dot(x, w_gate[b * piece : (b + 1) * piece, :])
            up_part = up_part + dot(x, w_up[b * piece : (b + 1) * piece, :])
        hidden[block] = (jax.nn.silu(gate_part) * up_part).astype(BF16)

    def contract(block, p):
        for b in range(cuts):
            start = b * piece + p * wide
            y = dot(hidden[block], w_down[:, start : start + wide]).reshape(pair, each, wide)
            for n in range(pair):
                partial[block * pair + n, p, b * each : (b + 1) * each, :] = y[n]
                part_out[block * pair + n, p, b * each : (b + 1) * each, :] = y[n].astype(BF16)

    def over(fn):
        if blocks == 1:
            fn(0)
        else:
            pl.loop(0, blocks)(fn)

    order_back = (
        lax.rem(q, each) // cap * TILE + q // each * cap + lax.rem(q, cap) == r
    ).astype(BF16)

    def collect(p):
        total = partial[lane, p]
        for j, mate in enumerate(mates):
            pltpu.make_async_remote_copy(
                src_ref=part_out.at[mate, p],
                dst_ref=part_in.at[mate, p],
                send_sem=psend_sem.at[j, p],
                recv_sem=precv_sem.at[mate, p],
                device_id={"side": chip * members + mate},
                device_id_type=MESH,
            ).wait_recv()
            total = total + part_in[mate, p].astype(F32)
        back_out[p] = dot(order_back, total.astype(BF16)).astype(BF16).reshape(experts, TILE, wide)
        for d, other in enumerate(others):
            copy = pltpu.make_async_remote_copy(
                src_ref=back_out.at[p, other],
                dst_ref=back_in.at[p, chip],
                send_sem=rsend_sem.at[p, d],
                recv_sem=rrecv_sem.at[p, chip],
                device_id={"side": other * members + lane},
                device_id_type=MESH,
            )
            copy.start()
            sends.append(copy)
        back_in[p, chip] = back_out[p, chip]

    over(expand)
    for p in range(parts):
        over(functools.partial(contract, p=p))
        give(p)
        if p > 0:
            collect(p - 1)
    collect(parts - 1)

    for p in range(parts):
        for d, source in sources():
            pltpu.make_async_remote_copy(
                src_ref=back_out.at[p, source],
                dst_ref=back_in.at[p, source],
                send_sem=rsend_sem.at[p, d - 1],
                recv_sem=rrecv_sem.at[p, source],
                device_id={"side": source * members + lane},
                device_id_type=MESH,
            ).wait_recv()
        moe = dot(combine, back_in[p].reshape(rows, wide))
        for b in range(cuts):
            columns = slice(b * piece + p * wide, b * piece + (p + 1) * wide)
            out_ref[:, columns] = (mid[:, columns] + moe[b * seqs : (b + 1) * seqs]).astype(BF16)
    for copy in sends:
        copy.wait_send()


def on_device(
    query,
    new_key,
    new_value,
    key_cache,
    value_cache,
    lengths,
    residual,
    norm_gain,
    router,
    routes,
    w_gate,
    w_up,
    w_down,
):
    seqs, width = residual.shape
    experts = router.shape[1]
    side = lax.axis_size("side")
    members = side // experts
    cap = seqs // 2
    cuts = TILE // cap
    piece = width // cuts
    each = experts * cap
    rows = experts * TILE
    parts = piece // PART
    wide = piece // parts
    pair = min(2, members)
    heads = width // HD
    vmem = pl.BlockSpec(memory_space=pltpu.VMEM)
    hbm = pl.BlockSpec(memory_space=pltpu.HBM)
    dma = pltpu.SemaphoreType.DMA
    return pl.pallas_call(
        functools.partial(kernel, side),
        out_shape=pltpu.VMEM((seqs, width), BF16),
        in_specs=[hbm] * 13,
        out_specs=vmem,
        scratch_shapes=[
            pltpu.VMEM(query.shape, BF16),
            pltpu.VMEM(new_key.shape, BF16),
            pltpu.VMEM(new_value.shape, BF16),
            pltpu.SMEM(lengths.shape, jnp.int32),
            pltpu.VMEM(residual.shape, BF16),
            pltpu.VMEM(norm_gain.shape, BF16),
            pltpu.VMEM((experts, width), BF16),
            pltpu.VMEM((2, seqs), jnp.int32),
            pltpu.VMEM(key_cache.shape, BF16),
            pltpu.VMEM(value_cache.shape, BF16),
            pltpu.VMEM(w_gate.shape, BF16),
            pltpu.VMEM(w_up.shape, BF16),
            pltpu.VMEM(w_down.shape, BF16),
            pltpu.VMEM((seqs * heads, HD), F32),
            pltpu.VMEM((seqs * heads, HD), F32),
            pltpu.VMEM((experts, TILE, piece), BF16),
            pltpu.VMEM((members, experts, TILE, piece), BF16),
            pltpu.VMEM((members // pair, pair * each, w_gate.shape[1]), BF16),
            pltpu.VMEM((members, parts, rows, wide), F32),
            pltpu.VMEM((members, parts, rows, wide), BF16),
            pltpu.VMEM((members, parts, rows, wide), BF16),
            pltpu.VMEM((parts, experts, TILE, wide), BF16),
            pltpu.VMEM((parts, experts, TILE, wide), BF16),
            dma((13,)),
            dma((experts - 1,)),
            dma((experts,)),
            dma((members, experts)),
            dma((members, experts)),
            dma((members, parts)),
            dma((members, parts)),
            dma((parts, experts - 1)),
            dma((parts, experts)),
        ],
        compiler_params=pltpu.CompilerParams(
            collective_id=0, has_side_effects=True, vmem_limit_bytes=56 * 1024 * 1024
        ),
    )(
        *[
            pltpu.with_memory_space_constraint(x, pltpu.HBM)
            for x in (
                query,
                new_key,
                new_value,
                lengths,
                residual,
                norm_gain,
                router.T,
                routes.T,
                key_cache,
                value_cache,
                w_gate,
                w_up,
                w_down,
            )
        ]
    )


def solution(mesh):
    in_specs = (
        P(("groups", "side"), None),
        P(("groups", "side"), None),
        P(("groups", "side"), None),
        P(("groups", "side"), None, None),
        P(("groups", "side"), None, None),
        P(("groups", "side")),
        P(("groups", "side"), None),
        P(),
        P(),
        P(("groups", "side"), None),
        P(None, "side"),
        P(None, "side"),
        P("side", None),
    )
    out_specs = P(("groups", "side"), None)
    return jax.shard_map(
        on_device, mesh=mesh, in_specs=in_specs, out_specs=out_specs, check_vma=False
    )
```
